256 devices in a mesh: pipe: 16 (over z, core), expert: 16 (over y, x).
Axes of the slice: x: 4, y: 4, z: 8, core: 2. Of those that a mesh axis runs over, the one named last changes fastest.
Arguments:
- tokens: bfloat16 [64, 512, 7168], P('pipe', 'expert'), may hold values from -6 to 6
- up_weight: bfloat16 [16, 7168, 4096], P('pipe', None, 'expert'), may hold values from -0.0625 to 0.0625
- down_weight: bfloat16 [16, 4096, 7168], P('pipe', 'expert'), may hold values from -0.125 to 0.125
- route: int32 [4, 16, 512, 1], P(None, 'pipe', 'expert'), may hold values from 0 to 1; in each aligned block of 32 rows (0 to 31, 32 to 63, ..., all dimensions but the last counted through in order) at most 18 rows name the same one
- gates: float32 [4, 16, 512], P(None, 'pipe', 'expert'), may hold values from 0.3 to 1
Outputs:
- mixed: bfloat16 [64, 512, 7168], P('pipe', 'expert')
The draws below stay inside these ranges and needn't reach their ends.
Inputs may be any that keep to these rules, and one draw needn't show every extreme that they name: `route`: in every aligned block of 32 tokens along the flattened leading dimensions (one device's tokens of one micro-batch at one step), no expert is named by more than 18 tokens, and some blocks reach 18.
All inputs are finite; a program needn't handle non-finite values.
Results may differ from the reference program's by a relative error of at most 0.0035.
Values may be sent and summed in bfloat16 or wider, within the bound.
No kernel may reach another device: no remote copies, remote signals or barrier semaphores. Data moves between devices by JAX's collectives and lax.ppermute only.
A program may use at most 128 MiB of HBM per device.

```python
import math
import jax
import jax.numpy as jnp
import numpy as np
from jax import lax

D = 7168
EXP_FF = 2048
EXPERTS = 2
MB = 4
TICKS = 4
MB_ROWS = 32
CAP = 18
SLICES = 8
HID_DEV = 256
HIDDEN_ALL = 4096
MICRO = 64
ROWS = 512
N_PIPE = 16


def steps_of(own_key, extent, split, least, top_value):
    level = 1.0
    for dim, parts in split:
        heights = jax.random.uniform(jax.random.fold_in(jax.random.fold_in(own_key, 6), dim), (parts,), jnp.float32, least / len(split), top_value / len(split))
        level = level * jnp.repeat(jnp.exp(heights), extent[dim] // parts).reshape((-1,) + (1,) * (len(extent) - 1 - dim))
    return level


def assign_block(rng, own, number, rows, amount, top, reach, lean):
    sequence = jax.random.permutation(rng, amount)
    crowded, usual = shares(amount, rows * top, reach, lean, True), shares(amount, rows * top, reach, lean, False)
    places = jnp.arange(amount)

    def named(sizes, rotation):
        used = int((sizes > 0).sum())
        fixed = max(1, used // 4)
        shifted = fixed + (places - fixed + rotation * (used - fixed)) % max(1, amount - fixed)
        return jnp.zeros((amount,), jnp.int32).at[sequence[jnp.where(places < fixed, places, shifted)]].set(jnp.asarray(sizes, jnp.int32))

    sizes = jnp.where(number % 4 == 0, named(crowded, number // 4), named(usual, number - number // 4 - 1))
    mixed = jax.random.permutation(jax.random.fold_in(own, 3), amount)
    giver, taker = mixed[0:amount // 2 * 2:2], mixed[1:amount // 2 * 2:2]
    margin = jnp.minimum(sizes[giver] - 1, reach - sizes[taker]) // 2
    margin = jnp.where((giver == sequence[0]) | (taker == sequence[0]) | (sizes[taker] == 0), 0, jnp.maximum(margin, 0))
    shifted = jax.random.randint(jax.random.fold_in(own, 4), (amount // 2,), 0, 1 << 20) % (margin + 1)
    sizes = sizes.at[giver].add(-shifted).at[taker].add(shifted)
    labels = jnp.searchsorted(jnp.cumsum(sizes), jnp.arange(rows * top), side="right").astype(jnp.int32)
    table = labels.reshape(top, rows).T
    table = table[jax.random.permutation(jax.random.fold_in(own, 1), rows)]
    rotation = jax.random.randint(jax.random.fold_in(own, 2), (rows, 1), 0, top)
    return jnp.take_along_axis(table, (jnp.arange(top)[None, :] + rotation) % top, axis=1)


def shares(number_of, total, most, skew, full):
    weights = [(1 << 20) // math.isqrt(standing ** skew) + 1 for standing in range(1, number_of + 1)]
    largest = most if full else min(most, max(-(-total // number_of), total * weights[0] // sum(weights)))
    least = 1 if total - largest >= number_of - 1 else 0
    holding, rest = [largest] + [least] * (number_of - 1), total - largest - least * (number_of - 1)
    while rest > 0:
        movable = [i for i in range(1, number_of) if holding[i] < largest] or [i for i in range(1, number_of) if holding[i] < most]
        mass, left = sum([weights[i] for i in movable]), rest
        for i in movable:
            more = min(most - holding[i], max(1, left * weights[i] // mass), rest)
            holding[i] = holding[i] + more
            rest = rest - more
    return np.array(holding)


def centred(rng, shape, scale, limit, cuts=(), held_as=jnp.bfloat16):
    values = scale * jax.random.normal(rng, shape, jnp.float32)
    if cuts:
        values = values * steps_of(rng, shape, cuts, -0.22, 0.18)
    return jnp.clip(values, -limit, limit).astype(held_as)


def setup_inputs(seed: int = 0) -> dict:
    arg_keys = jax.random.split(jax.random.key(seed), 6)
    tokens = centred(arg_keys[0], (MICRO, ROWS, D), 1.0, 6.0, ((0, 16), (1, 16)))
    up_weight = centred(arg_keys[1], (N_PIPE, D, HIDDEN_ALL), D ** -0.5, 0.0625, ((0, 16), (2, 16)))
    down_weight = centred(arg_keys[2], (N_PIPE, HIDDEN_ALL, D), EXP_FF ** -0.5, 0.125, ((0, 16), (1, 16)))
    route_keys = jax.random.split(jax.random.fold_in(arg_keys[3], 1), TICKS * N_PIPE * ROWS // MB_ROWS)
    route_turns = jax.random.permutation(jax.random.fold_in(arg_keys[3], 3), TICKS * N_PIPE * ROWS // MB_ROWS)
    route = jax.vmap(lambda own, number: assign_block(jax.random.fold_in(arg_keys[3], 2), own, number, MB_ROWS, EXPERTS, 1, CAP, 2))(route_keys, route_turns).reshape((TICKS, N_PIPE, ROWS, 1))
    gates = jnp.clip(jnp.exp(math.log(1.0) - 1.2039728 * jax.random.uniform(arg_keys[4], (TICKS, N_PIPE, ROWS), jnp.float32) ** steps_of(arg_keys[4], (TICKS, N_PIPE, ROWS), ((1, 16), (2, 16)), -0.2, 0.2)), 0.3, 1.0)
    return dict(tokens=tokens, up_weight=up_weight, down_weight=down_weight, route=route, gates=gates)


epsilon = 1e-06

def normalize(tok_rows):
    widened = tok_rows.astype(jnp.float32)
    inverse_rms = lax.rsqrt(lax.optimization_barrier(jnp.mean(widened * widened, axis=-1, keepdims=True)) + epsilon)
    return (widened * inverse_rms).astype(jnp.bfloat16)

def section_update(packed):
    tok_rows, up_section, down_section, expert_ids, gate_rows = packed
    normed = normalize(tok_rows)
    summed_out = jnp.zeros(tok_rows.shape, jnp.float32)
    for expert in range(EXPERTS):
        up_block = up_section[:, expert * EXP_FF:(expert + 1) * EXP_FF]
        hidden = jax.nn.silu(jnp.dot(normed, up_block, preferred_element_type=jnp.float32)).astype(jnp.bfloat16)
        down_block = down_section[expert * EXP_FF:(expert + 1) * EXP_FF].reshape(SLICES, HID_DEV, D)
        pieces = jnp.einsum('rsh,shd->rsd', hidden.reshape(-1, SLICES, HID_DEV).astype(jnp.float32), down_block.astype(jnp.float32))
        rounded = lax.optimization_barrier(pieces.astype(jnp.bfloat16))
        summed = lax.optimization_barrier(jnp.sum(rounded.astype(jnp.float32), axis=1))
        picked = (expert_ids == expert)[:, None]
        summed_out = jnp.where(picked, summed, summed_out)
    return (tok_rows.astype(jnp.float32) + gate_rows[:, None] * summed_out).astype(jnp.bfloat16)

def reference(tokens, up_weight, down_weight, route, gates):
    stream = tokens.reshape(N_PIPE, MB, ROWS, D)
    for tick_index in range(TICKS):
        slot_index = tick_index % MB
        current = stream[:, slot_index]
        updated = lax.map(section_update, (current, up_weight, down_weight, route[tick_index, :, :, 0], gates[tick_index]))
        stream = stream.at[:, slot_index].set(jnp.roll(updated, 1, axis=0))
    return stream.reshape(MICRO, ROWS, D)
```

```python
import jax
import jax.numpy as jnp
from jax import lax
from jax.sharding import PartitionSpec as P

D = 7168
EXPERTS = 2
CAP = 18
SIDE = 4
PART = D // SIDE

epsilon = 1e-06


def shift(block, dy, dx):
    pairs = []
    for y in range(SIDE):
        for x in range(SIDE):
            pairs.append((y * SIDE + x, (y + dy) % SIDE * SIDE + (x + dx) % SIDE))
    return lax.ppermute(block, "expert", pairs)


def shift_on(block, dx):
    count = lax.axis_size("pipe")
    pairs = []
    for p in range(count):
        for y in range(SIDE):
            for x in range(SIDE):
                source = p * SIDE * SIDE + y * SIDE + x
                target = (p + 1) % count * SIDE * SIDE + y * SIDE + (x + dx) % SIDE
                pairs.append((source, target))
    return lax.ppermute(block, ("pipe", "expert"), pairs)


def normalize(tok_rows):
    widened = tok_rows.astype(jnp.float32)
    inverse_rms = lax.rsqrt(jnp.mean(widened * widened, axis=-1, keepdims=True) + epsilon)
    return (widened * inverse_rms).astype(jnp.bfloat16)


def slots_of(ids, own, slots):
    rel = (ids != own).astype(jnp.int32)
    count = ids.shape[0]
    member = (rel[:, None] == jnp.arange(EXPERTS, dtype=jnp.int32)[None, :]).astype(jnp.bfloat16)
    earlier = jnp.arange(count)[:, None] > jnp.arange(count)[None, :]
    before = jnp.dot(earlier.astype(jnp.bfloat16), member, preferred_element_type=jnp.float32)
    rank = jnp.sum(before * member.astype(jnp.float32), axis=1).astype(jnp.int32)
    return rel * slots + rank


def turn(block, step, slots):
    split = block.reshape(SIDE, SIDE, slots, -1)
    return jnp.roll(split, step, axis=1).reshape(block.shape)


def after(value, *done):
    zero = value
    for d in done:
        first = d.reshape(-1)[0].astype(jnp.float32)
        zero = zero + jnp.minimum(jnp.abs(first).astype(jnp.int32), 0)
    return zero


def per_device(tokens, up_weight, down_weight, route, gates):
    ticks, _, block, _ = route.shape
    count = ticks * block
    slots = ticks * CAP
    place = lax.axis_index("expert")
    y, x = place // SIDE, place % SIDE
    even = y % 2 == 0
    own = y // 2
    up_local, down_local = up_weight[0], down_weight[0]
    rows = tokens.reshape(count, D)

    def quarter(step):
        return (x + step) % SIDE * PART

    rows_before = shift_on(rows, 0)
    route_before = shift_on(route.reshape(count), 0)
    gates_before = shift_on(gates.reshape(count), 0)

    slot = slots_of(route.reshape(count), own, slots)
    lanes = jnp.arange(EXPERTS * slots, dtype=jnp.int32)
    table = (lanes[:, None] == slot[None, :]).astype(jnp.bfloat16)
    normed = normalize(rows)

    from_x = []
    for step in range(SIDE):
        part = lax.dynamic_slice(normed, (0, quarter(step)), (count, PART))
        message = jnp.dot(table, part, preferred_element_type=jnp.float32).astype(jnp.bfloat16)
        from_x.append(shift(message, 0, step) if step else message)

    zero = after(jnp.int32(0), *from_x[1:])
    ups = []
    for step in range(SIDE):
        piece = lax.dynamic_slice(up_local, (quarter(step) + zero, 0), (PART, up_local.shape[1]))
        ups.append(shift(piece, 0, step) if step else piece)

    ours = jnp.stack([r[:slots] for r in from_x])
    theirs = jnp.stack([r[slots:] for r in from_x])
    sent = [ours, jnp.where(even, ours, theirs), theirs, jnp.where(even, theirs, ours)]
    from_y = [shift(m, step, 0) if step else m for step, m in enumerate(sent)]
    received = jnp.stack(from_y).reshape(-1, PART)

    zero = after(jnp.int32(0), *ups[1:])
    downs = []
    for step in range(SIDE):
        piece = lax.dynamic_slice(down_local, (0, quarter(step) + zero), (down_local.shape[0], PART))
        downs.append(shift(piece, 0, step) if step else piece)

    value = 0.0
    for step in range(SIDE):
        partial = jnp.dot(received, ups[step], preferred_element_type=jnp.float32)
        if step:
            partial = shift(turn(partial.astype(jnp.bfloat16), -step, slots), 0, -step)
        value = value + partial.astype(jnp.float32)
    hidden = jax.nn.silu(value).astype(jnp.bfloat16)

    out = 0.0
    for step in range(SIDE):
        arrived = shift(turn(hidden, step, slots), 0, step) if step else hidden
        out = out + jnp.dot(arrived, downs[step], preferred_element_type=jnp.float32)
    out = out.astype(jnp.bfloat16).reshape(SIDE, SIDE, slots, PART)

    back = [(shift(out[step], -step, 0) if step else out[0]).astype(jnp.float32) for step in range(SIDE)]
    ours = (back[0] + jnp.where(even, back[1], back[3])).astype(jnp.bfloat16)
    theirs = (back[2] + jnp.where(even, back[3], back[1])).astype(jnp.bfloat16)

    slot = slots_of(route_before, own, slots)
    table = (slot[:, None] == lanes[None, :]).astype(jnp.bfloat16)
    result = jnp.zeros((count, D), jnp.bfloat16)
    for step in range(SIDE):
        message = jnp.concatenate([ours[step], theirs[step]])
        arrived = shift_on(message, -step)
        combined = jnp.dot(table, arrived, preferred_element_type=jnp.float32)
        part = lax.dynamic_slice(rows_before, (0, quarter(step)), (count, PART))
        updated = part.astype(jnp.float32) + gates_before[:, None] * combined
        result = lax.dynamic_update_slice(result, updated.astype(jnp.bfloat16), (0, quarter(step)))
    return result.reshape(tokens.shape)


def solution(mesh):
    in_specs = (
        P("pipe", "expert", None),
        P("pipe", None, "expert"),
        P("pipe", "expert", None),
        P(None, "pipe", "expert", None),
        P(None, "pipe", "expert"),
    )
    out_specs = P("pipe", "expert", None)
    return jax.shard_map(
        per_device, mesh=mesh, in_specs=in_specs, out_specs=out_specs, check_vma=False
    )
```

```python
import jax
import jax.numpy as jnp
from jax import lax
from jax.sharding import PartitionSpec as P

D = 7168
EXPERTS = 2
CAP = 18
SIDE = 4
PART = D // SIDE
CUTS = (40, 32)

epsilon = 1e-06


def shift(block, dy, dx):
    pairs = []
    for y in range(SIDE):
        for x in range(SIDE):
            pairs.append((y * SIDE + x, (y + dy) % SIDE * SIDE + (x + dx) % SIDE))
    return lax.ppermute(block, "expert", pairs)


def shift_on(block, dx):
    count = lax.axis_size("pipe")
    pairs = []
    for p in range(count):
        for y in range(SIDE):
            for x in range(SIDE):
                source = p * SIDE * SIDE + y * SIDE + x
                target = (p + 1) % count * SIDE * SIDE + y * SIDE + (x + dx) % SIDE
                pairs.append((source, target))
    return lax.ppermute(block, ("pipe", "expert"), pairs)


def normalize(tok_rows):
    widened = tok_rows.astype(jnp.float32)
    inverse_rms = lax.rsqrt(jnp.mean(widened * widened, axis=-1, keepdims=True) + epsilon)
    return (widened * inverse_rms).astype(jnp.bfloat16)


def slots_of(ids, own):
    rel = (ids != own).astype(jnp.int32)
    count = ids.shape[0]
    member = (rel[:, None] == jnp.arange(EXPERTS, dtype=jnp.int32)[None, :]).astype(jnp.bfloat16)
    earlier = jnp.arange(count)[:, None] > jnp.arange(count)[None, :]
    before = jnp.dot(earlier.astype(jnp.bfloat16), member, preferred_element_type=jnp.float32)
    rank = jnp.sum(before * member.astype(jnp.float32), axis=1).astype(jnp.int32)
    slot, first = 0 * rank, 0
    for size in CUTS:
        inside = (rank >= first) & (rank < first + size)
        slot = jnp.where(inside, EXPERTS * first + rel * size + rank - first, slot)
        first += size
    return slot


def turn(block, step, slots):
    split = block.reshape(SIDE, SIDE, slots, -1)
    return jnp.roll(split, step, axis=1).reshape(block.shape)


def tie(value, *done):
    return lax.optimization_barrier((value, *done))[0]


def exchange(pieces):
    groups = [[y * SIDE + x for x in range(SIDE)] for y in range(SIDE)]
    return lax.all_to_all(pieces, "expert", 0, 0, axis_index_groups=groups, tiled=True)


def per_device(tokens, up_weight, down_weight, route, gates):
    ticks, _, block, _ = route.shape
    count = ticks * block
    assert sum(CUTS) == ticks * CAP
    place = lax.axis_index("expert")
    y, x = place // SIDE, place % SIDE
    even = y % 2 == 0
    own = y // 2
    up_local, down_local = up_weight[0], down_weight[0]
    depth = up_local.shape[1]
    rows = tokens.reshape(count, D)
    starts = [EXPERTS * sum(CUTS[:c]) for c in range(len(CUTS))]
    cuts = range(len(CUTS))

    def quarter(step):
        return (x + step) % SIDE * PART

    def of(pieces, step):
        return lax.dynamic_index_in_dim(pieces, (x + step) % SIDE, 0, keepdims=False)

    ups = exchange(up_local.reshape(SIDE, PART, depth))
    downs = exchange(jnp.transpose(down_local.reshape(depth, SIDE, PART), (1, 0, 2)))

    slot = slots_of(route.reshape(count), own)
    lanes = jnp.arange(EXPERTS * ticks * CAP, dtype=jnp.int32)
    table = (lanes[:, None] == slot[None, :]).astype(jnp.bfloat16)
    normed = normalize(rows)

    from_x = []
    for step in range(SIDE):
        part = lax.dynamic_slice(normed, (0, quarter(step)), (count, PART))
        message = jnp.dot(table, part, preferred_element_type=jnp.float32).astype(jnp.bfloat16)
        from_x.append(shift(message, 0, step) if step else message)

    received = []
    for c in cuts:
        ours = jnp.stack([r[starts[c] : starts[c] + CUTS[c]] for r in from_x])
        theirs = jnp.stack([r[starts[c] + CUTS[c] : starts[c] + EXPERTS * CUTS[c]] for r in from_x])
        if c:
            ours = tie(ours, ups)
            theirs = tie(theirs, ups)
        sent = [ours, jnp.where(even, ours, theirs), theirs, jnp.where(even, theirs, ours)]
        from_y = [shift(m, step, 0) if step else m for step, m in enumerate(sent)]
        received.append(jnp.stack(from_y).reshape(-1, PART))

    facts = jnp.stack([slot.astype(jnp.float32), gates.reshape(count)])
    rows_before = shift_on(tie(rows, received[0]), 0)
    facts_before = shift_on(tie(facts, received[0]), 0)

    value = 0.0
    for step in range(SIDE):
        partial = []
        for c in cuts:
            product = jnp.dot(received[c], of(ups, -step), preferred_element_type=jnp.float32)
            partial.append(turn(product.astype(jnp.bfloat16), -step, CUTS[c]) if step else product)
        partial = jnp.concatenate(partial)
        if step:
            partial = shift(partial, 0, -step)
        value = value + partial.astype(jnp.float32)
    hidden = jax.nn.silu(tie(value, rows_before, facts_before)).astype(jnp.bfloat16)
    edges = [SIDE * SIDE * sum(CUTS[:c]) for c in range(len(CUTS) + 1)]
    hiddens = [hidden[edges[c] : edges[c + 1]] for c in cuts]

    slot = facts_before[0].astype(jnp.int32)
    table = (slot[:, None] == lanes[None, :]).astype(jnp.bfloat16)
    combined = [0.0] * SIDE
    for c in cuts:
        out = 0.0
        for step in range(SIDE):
            arrived = shift(turn(hiddens[c], step, CUTS[c]), 0, step) if step else hiddens[c]
            out = out + jnp.dot(arrived, of(downs, -step), preferred_element_type=jnp.float32)
        out = out.astype(jnp.bfloat16).reshape(SIDE, SIDE, CUTS[c], PART)

        back = [(shift(out[step], -step, 0) if step else out[0]).astype(jnp.float32) for step in range(SIDE)]
        ours = (back[0] + jnp.where(even, back[1], back[3])).astype(jnp.bfloat16)
        theirs = (back[2] + jnp.where(even, back[3], back[1])).astype(jnp.bfloat16)
        for step in range(SIDE):
            message = jnp.concatenate([ours[step], theirs[step]])
            arrived = shift_on(message, -step)
            chosen = table[:, starts[c] : starts[c] + EXPERTS * CUTS[c]]
            combined[step] = combined[step] + jnp.dot(chosen, arrived, preferred_element_type=jnp.float32)

    result = jnp.zeros((count, D), jnp.bfloat16)
    for step in range(SIDE):
        part = lax.dynamic_slice(rows_before, (0, quarter(step)), (count, PART))
        updated = part.astype(jnp.float32) + facts_before[1][:, None] * combined[step]
        result = lax.dynamic_update_slice(result, updated.astype(jnp.bfloat16), (0, quarter(step)))
    return result.reshape(tokens.shape)


def solution(mesh):
    in_specs = (
        P("pipe", "expert", None),
        P("pipe", None, "expert"),
        P("pipe", "expert", None),
        P(None, "pipe", "expert", None),
        P(None, "pipe", "expert"),
    )
    out_specs = P("pipe", "expert", None)
    return jax.shard_map(
        per_device, mesh=mesh, in_specs=in_specs, out_specs=out_specs, check_vma=False
    )
```

```python
import jax
import jax.numpy as jnp
from jax import lax
from jax.sharding import PartitionSpec as P

D = 7168
EXPERTS = 2
CAP = 18
SIDE = 4
PART = D // SIDE
HALF = PART // 2

epsilon = 1e-06


def shift(block, dy, dx):
    pairs = []
    for y in range(SIDE):
        for x in range(SIDE):
            pairs.append((y * SIDE + x, (y + dy) % SIDE * SIDE + (x + dx) % SIDE))
    return lax.ppermute(block, "expert", pairs)


def shift_on(block, dx):
    count = lax.axis_size("pipe")
    pairs = []
    for p in range(count):
        for y in range(SIDE):
            for x in range(SIDE):
                source = p * SIDE * SIDE + y * SIDE + x
                target = (p + 1) % count * SIDE * SIDE + y * SIDE + (x + dx) % SIDE
                pairs.append((source, target))
    return lax.ppermute(block, ("pipe", "expert"), pairs)


def normalize(tok_rows):
    widened = tok_rows.astype(jnp.float32)
    inverse_rms = lax.rsqrt(jnp.mean(widened * widened, axis=-1, keepdims=True) + epsilon)
    return (widened * inverse_rms).astype(jnp.bfloat16)


def slots_of(ids, own, slots):
    rel = (ids != own).astype(jnp.int32)
    count = ids.shape[0]
    member = (rel[:, None] == jnp.arange(EXPERTS, dtype=jnp.int32)[None, :]).astype(jnp.bfloat16)
    earlier = jnp.arange(count)[:, None] > jnp.arange(count)[None, :]
    before = jnp.dot(earlier.astype(jnp.bfloat16), member, preferred_element_type=jnp.float32)
    rank = jnp.sum(before * member.astype(jnp.float32), axis=1).astype(jnp.int32)
    return rel * slots + rank


def turn(block, step, slots):
    split = block.reshape(SIDE, SIDE, slots, -1)
    return jnp.roll(split, step, axis=1).reshape(block.shape)


def tie(value, *done):
    return lax.optimization_barrier((value, *done))[0]


def exchange(pieces):
    groups = [[y * SIDE + x for x in range(SIDE)] for y in range(SIDE)]
    return lax.all_to_all(pieces, "expert", 0, 0, axis_index_groups=groups, tiled=True)


def per_device(tokens, up_weight, down_weight, route, gates):
    ticks, _, block, _ = route.shape
    count = ticks * block
    slots = ticks * CAP
    place = lax.axis_index("expert")
    y, x = place // SIDE, place % SIDE
    even = y % 2 == 0
    own = y // 2
    up_local, down_local = up_weight[0], down_weight[0]
    depth = up_local.shape[1]
    rows = tokens.reshape(count, D)
    halves = range(2)

    def quarter(step):
        return (x + step) % SIDE * PART

    def of(pieces, index):
        return lax.dynamic_index_in_dim(pieces, index % SIDE, 0, keepdims=False)

    pieces = jnp.transpose(down_local.reshape(depth, SIDE, 2, HALF), (2, 1, 0, 3))

    slot = slots_of(route.reshape(count), own, slots)
    lanes = jnp.arange(EXPERTS * slots, dtype=jnp.int32)
    table = (lanes[:, None] == slot[None, :]).astype(jnp.bfloat16)
    normed = normalize(rows)

    from_x = []
    for step in range(SIDE):
        part = lax.dynamic_slice(normed, (0, quarter(step)), (count, PART))
        message = jnp.dot(table, part, preferred_element_type=jnp.float32).astype(jnp.bfloat16)
        from_x.append(shift(message, 0, step) if step else message)

    ups = exchange(tie(up_local, message).reshape(SIDE, PART, depth))
    downs = [exchange(pieces[0])]

    received = []
    for h in halves:
        columns = slice(h * HALF, (h + 1) * HALF)
        ours = jnp.stack([r[:slots, columns] for r in from_x])
        theirs = jnp.stack([r[slots:, columns] for r in from_x])
        sent = [ours, jnp.where(even, ours, theirs), theirs, jnp.where(even, theirs, ours)]
        if h:
            sent[3] = tie(sent[3], ups)
        from_y = [shift(m, step, 0) if step else m for step, m in enumerate(sent)]
        received.append(jnp.stack(from_y).reshape(-1, HALF))

    facts = jnp.stack([slot.astype(jnp.float32), gates.reshape(count)])
    rows_before = shift_on(tie(rows, received[1]), 0)
    facts_before = shift_on(tie(facts, received[1]), 0)

    value = 0.0
    for step in range(SIDE):
        up = of(ups, x - step)
        partial = 0.0
        for h in halves:
            partial = partial + jnp.dot(
                received[h], up[h * HALF : (h + 1) * HALF], preferred_element_type=jnp.float32
            )
        if step:
            partial = tie(partial, downs[0])
            partial = shift(turn(partial.astype(jnp.bfloat16), -step, slots), 0, -step)
        value = value + partial.astype(jnp.float32)
    hidden = jax.nn.silu(tie(value, rows_before, facts_before)).astype(jnp.bfloat16)
    gathered = [shift(turn(hidden, step, slots), 0, step) if step else hidden for step in range(SIDE)]
    downs.append(exchange(tie(pieces[1], *gathered)))

    slot = facts_before[0].astype(jnp.int32)
    table = (slot[:, None] == lanes[None, :]).astype(jnp.bfloat16)
    result = jnp.zeros((count, D), jnp.bfloat16)
    for h in halves:
        out = 0.0
        for step in range(SIDE):
            down = of(downs[h], x - step)
            out = out + jnp.dot(gathered[step], down, preferred_element_type=jnp.float32)
        out = out.astype(jnp.bfloat16).reshape(SIDE, SIDE, slots, HALF)
        back = [(shift(out[step], -step, 0) if step else out[0]).astype(jnp.float32) for step in range(SIDE)]
        ours = (back[0] + jnp.where(even, back[1], back[3])).astype(jnp.bfloat16)
        theirs = (back[2] + jnp.where(even, back[3], back[1])).astype(jnp.bfloat16)
        for step in range(SIDE):
            message = jnp.concatenate([ours[step], theirs[step]])
            arrived = shift_on(message, -step)
            combined = jnp.dot(table, arrived, preferred_element_type=jnp.float32)
            place = (0, quarter(step) + h * HALF)
            part = lax.dynamic_slice(rows_before, place, (count, HALF))
            updated = part.astype(jnp.float32) + facts_before[1][:, None] * combined
            result = lax.dynamic_update_slice(result, updated.astype(jnp.bfloat16), place)
    return result.reshape(tokens.shape)


def solution(mesh):
    in_specs = (
        P("pipe", "expert", None),
        P("pipe", None, "expert"),
        P("pipe", "expert", None),
        P(None, "pipe", "expert", None),
        P(None, "pipe", "expert"),
    )
    out_specs = P("pipe", "expert", None)
    return jax.shard_map(
        per_device, mesh=mesh, in_specs=in_specs, out_specs=out_specs, check_vma=False
    )
```

```python
import jax
import jax.numpy as jnp
from jax import lax
from jax.sharding import PartitionSpec as P

D = 7168
EXPERTS = 2
CAP = 18
SIDE = 4
PART = D // SIDE
HALF = PART // 2

epsilon = 1e-06


def shift(block, dy, dx):
    pairs = []
    for y in range(SIDE):
        for x in range(SIDE):
            pairs.append((y * SIDE + x, (y + dy) % SIDE * SIDE + (x + dx) % SIDE))
    return lax.ppermute(block, "expert", pairs)


def shift_on(block, dx):
    count = lax.axis_size("pipe")
    pairs = []
    for p in range(count):
        for y in range(SIDE):
            for x in range(SIDE):
                source = p * SIDE * SIDE + y * SIDE + x
                target = (p + 1) % count * SIDE * SIDE + y * SIDE + (x + dx) % SIDE
                pairs.append((source, target))
    return lax.ppermute(block, ("pipe", "expert"), pairs)


def normalize(tok_rows):
    widened = tok_rows.astype(jnp.float32)
    inverse_rms = lax.rsqrt(jnp.mean(widened * widened, axis=-1, keepdims=True) + epsilon)
    return (widened * inverse_rms).astype(jnp.bfloat16)


def slots_of(ids, own, slots):
    rel = (ids != own).astype(jnp.int32)
    count = ids.shape[0]
    member = (rel[:, None] == jnp.arange(EXPERTS, dtype=jnp.int32)[None, :]).astype(jnp.bfloat16)
    earlier = jnp.arange(count)[:, None] > jnp.arange(count)[None, :]
    before = jnp.dot(earlier.astype(jnp.bfloat16), member, preferred_element_type=jnp.float32)
    rank = jnp.sum(before * member.astype(jnp.float32), axis=1).astype(jnp.int32)
    return rel * slots + rank


def turn(block, step, slots):
    split = block.reshape(SIDE, SIDE, slots, -1)
    return jnp.roll(split, step, axis=1).reshape(block.shape)


def tie(value, *done):
    return lax.optimization_barrier((value, *done))[0]


def exchange(pieces):
    groups = [[y * SIDE + x for x in range(SIDE)] for y in range(SIDE)]
    return lax.all_to_all(pieces, "expert", 0, 0, axis_index_groups=groups, tiled=True)


def per_device(tokens, up_weight, down_weight, route, gates):
    ticks, _, block, _ = route.shape
    count = ticks * block
    slots = ticks * CAP
    place = lax.axis_index("expert")
    y, x = place // SIDE, place % SIDE
    even = y % 2 == 0
    own = y // 2
    up_local, down_local = up_weight[0], down_weight[0]
    depth = up_local.shape[1]
    rows = tokens.reshape(count, D)
    halves = range(2)

    def quarter(step):
        return (x + step) % SIDE * PART

    def of(pieces, index):
        return lax.dynamic_index_in_dim(pieces, index % SIDE, 0, keepdims=False)

    edges = [[part * PART + h * HALF for part in range(SIDE)] for h in halves]
    pieces = [jnp.stack([down_local[:, edge : edge + HALF] for edge in edges[h]]) for h in halves]

    slot = slots_of(route.reshape(count), own, slots)
    lanes = jnp.arange(EXPERTS * slots, dtype=jnp.int32)
    table = (lanes[:, None] == slot[None, :]).astype(jnp.bfloat16)
    normed = normalize(rows)

    from_x = []
    for step in range(SIDE):
        part = lax.dynamic_slice(normed, (0, quarter(step)), (count, PART))
        message = jnp.dot(table, part, preferred_element_type=jnp.float32).astype(jnp.bfloat16)
        from_x.append(shift(message, 0, step) if step else message)

    ups = exchange(tie(up_local, *from_x[1:]).reshape(SIDE, PART, depth))
    downs = [exchange(pieces[0])]

    received = []
    for h in halves:
        columns = slice(h * HALF, (h + 1) * HALF)
        ours = jnp.stack([r[:slots, columns] for r in from_x])
        theirs = jnp.stack([r[slots:, columns] for r in from_x])
        sent = [ours, jnp.where(even, ours, theirs), theirs, jnp.where(even, theirs, ours)]
        if h:
            sent[3] = tie(sent[3], ups)
        from_y = [shift(m, step, 0) if step else m for step, m in enumerate(sent)]
        received.append(jnp.stack(from_y).reshape(-1, HALF))

    facts = jnp.stack([slot.astype(jnp.float32), gates.reshape(count)])
    rows_before = shift_on(tie(rows, received[1]), 0)
    facts_before = shift_on(tie(facts, received[1]), 0)

    value = 0.0
    for step in range(SIDE):
        up = of(ups, x - step)
        partial = 0.0
        for h in halves:
            partial = partial + jnp.dot(
                received[h], up[h * HALF : (h + 1) * HALF], preferred_element_type=jnp.float32
            )
        if step:
            partial = tie(partial, downs[0])
            partial = shift(turn(partial.astype(jnp.bfloat16), -step, slots), 0, -step)
        value = value + partial.astype(jnp.float32)
    hidden = jax.nn.silu(tie(value, rows_before, facts_before)).astype(jnp.bfloat16)
    gathered = [shift(turn(hidden, step, slots), 0, step) if step else hidden for step in range(SIDE)]
    downs.append(exchange(tie(pieces[1], gathered[2])))

    slot = facts_before[0].astype(jnp.int32)
    table = (slot[:, None] == lanes[None, :]).astype(jnp.bfloat16)
    result = jnp.zeros((count, D), jnp.bfloat16)
    landed = []
    for h in halves:
        out = 0.0
        for step in range(SIDE):
            down = of(downs[h], x - step)
            out = out + jnp.dot(gathered[step], down, preferred_element_type=jnp.float32)
        out = out.astype(jnp.bfloat16).reshape(SIDE, SIDE, slots, HALF)
        back = [shift(out[step], -step, 0) if step else out[0] for step in range(SIDE)]
        if h:
            back = [tie(b, ours, theirs) for b in back]
        else:
            back = [tie(b, downs[1]) for b in back]
        back = [b.astype(jnp.float32) for b in back]
        ours = (back[0] + jnp.where(even, back[1], back[3])).astype(jnp.bfloat16)
        theirs = (back[2] + jnp.where(even, back[3], back[1])).astype(jnp.bfloat16)
        messages = [jnp.concatenate([ours[step], theirs[step]]) for step in range(SIDE)]
        if h:
            messages = [tie(message, *landed) for message in messages]
        landed = [shift_on(message, -step) for step, message in enumerate(messages)]
        for step in range(SIDE):
            combined = jnp.dot(table, landed[step], preferred_element_type=jnp.float32)
            place = (0, quarter(step) + h * HALF)
            part = lax.dynamic_slice(rows_before, place, (count, HALF))
            updated = part.astype(jnp.float32) + facts_before[1][:, None] * combined
            result = lax.dynamic_update_slice(result, updated.astype(jnp.bfloat16), place)
    return result.reshape(tokens.shape)


def solution(mesh):
    in_specs = (
        P("pipe", "expert", None),
        P("pipe", None, "expert"),
        P("pipe", "expert", None),
        P(None, "pipe", "expert", None),
        P(None, "pipe", "expert"),
    )
    out_specs = P("pipe", "expert", None)
    return jax.shard_map(
        per_device, mesh=mesh, in_specs=in_specs, out_specs=out_specs, check_vma=False
    )
```

```python
import jax
import jax.numpy as jnp
from jax import lax
from jax.sharding import PartitionSpec as P

D = 7168
EXPERTS = 2
CAP = 18
SIDE = 4
PART = D // SIDE
CUTS = (40, 32)

epsilon = 1e-06


def shift(block, dy, dx):
    pairs = []
    for y in range(SIDE):
        for x in range(SIDE):
            pairs.append((y * SIDE + x, (y + dy) % SIDE * SIDE + (x + dx) % SIDE))
    return lax.ppermute(block, "expert", pairs)


def shift_on(block, dx):
    count = lax.axis_size("pipe")
    pairs = []
    for p in range(count):
        for y in range(SIDE):
            for x in range(SIDE):
                source = p * SIDE * SIDE + y * SIDE + x
                target = (p + 1) % count * SIDE * SIDE + y * SIDE + (x + dx) % SIDE
                pairs.append((source, target))
    return lax.ppermute(block, ("pipe", "expert"), pairs)


def normalize(tok_rows):
    widened = tok_rows.astype(jnp.float32)
    inverse_rms = lax.rsqrt(jnp.mean(widened * widened, axis=-1, keepdims=True) + epsilon)
    return (widened * inverse_rms).astype(jnp.bfloat16)


def slots_of(ids, own):
    rel = (ids != own).astype(jnp.int32)
    count = ids.shape[0]
    member = (rel[:, None] == jnp.arange(EXPERTS, dtype=jnp.int32)[None, :]).astype(jnp.bfloat16)
    earlier = jnp.arange(count)[:, None] > jnp.arange(count)[None, :]
    before = jnp.dot(earlier.astype(jnp.bfloat16), member, preferred_element_type=jnp.float32)
    rank = jnp.sum(before * member.astype(jnp.float32), axis=1).astype(jnp.int32)
    slot, first = 0 * rank, 0
    for size in CUTS:
        inside = (rank >= first) & (rank < first + size)
        slot = jnp.where(inside, EXPERTS * first + rel * size + rank - first, slot)
        first += size
    return slot


def turn(block, step, slots):
    split = block.reshape(SIDE, SIDE, slots, -1)
    return jnp.roll(split, step, axis=1).reshape(block.shape)


def tie(value, *done):
    return lax.optimization_barrier((value, *done))[0]


def exchange(pieces, along_y=False):
    groups = [[y * SIDE + x for x in range(SIDE)] for y in range(SIDE)]
    if along_y:
        groups = [list(group) for group in zip(*groups)]
    return lax.all_to_all(pieces, "expert", 0, 0, axis_index_groups=groups, tiled=True)


def per_device(tokens, up_weight, down_weight, route, gates):
    ticks, _, block, _ = route.shape
    count = ticks * block
    assert sum(CUTS) == ticks * CAP
    place = lax.axis_index("expert")
    y, x = place // SIDE, place % SIDE
    even = y % 2 == 0
    own = y // 2
    up_local, down_local = up_weight[0], down_weight[0]
    depth = up_local.shape[1]
    rows = tokens.reshape(count, D)
    starts = [EXPERTS * sum(CUTS[:c]) for c in range(len(CUTS))]
    cuts = range(len(CUTS))

    def quarter(step):
        return (x + step) % SIDE * PART

    def of(pieces, step):
        return lax.dynamic_index_in_dim(pieces, (x + step) % SIDE, 0, keepdims=False)

    ups = exchange(up_local.reshape(SIDE, PART, depth))
    downs = exchange(jnp.transpose(down_local.reshape(depth, SIDE, PART), (1, 0, 2)))

    slot = slots_of(route.reshape(count), own)
    lanes = jnp.arange(EXPERTS * ticks * CAP, dtype=jnp.int32)
    table = (lanes[:, None] == slot[None, :]).astype(jnp.bfloat16)
    normed = normalize(rows)

    from_x = []
    for step in range(SIDE):
        part = lax.dynamic_slice(normed, (0, quarter(step)), (count, PART))
        message = jnp.dot(table, part, preferred_element_type=jnp.float32).astype(jnp.bfloat16)
        from_x.append(shift(message, 0, step) if step else message)

    received = []
    for c in cuts:
        ours = jnp.stack([r[starts[c] : starts[c] + CUTS[c]] for r in from_x])
        theirs = jnp.stack([r[starts[c] + CUTS[c] : starts[c] + EXPERTS * CUTS[c]] for r in from_x])
        if c:
            ours = tie(ours, ups)
            theirs = tie(theirs, ups)
        sent = [ours, jnp.where(even, ours, theirs), theirs, jnp.where(even, theirs, ours)]
        from_y = [shift(m, step, 0) if step else m for step, m in enumerate(sent)]
        received.append(jnp.stack(from_y).reshape(-1, PART))

    facts = jnp.stack([slot.astype(jnp.float32), gates.reshape(count)])
    rows_before = shift_on(tie(rows, received[0]), 0)
    facts_before = shift_on(tie(facts, received[0]), 0)

    value = 0.0
    for step in range(SIDE):
        partial = []
        for c in cuts:
            product = jnp.dot(received[c], of(ups, -step), preferred_element_type=jnp.float32)
            partial.append(turn(product.astype(jnp.bfloat16), -step, CUTS[c]) if step else product)
        partial = jnp.concatenate(partial)
        if step:
            partial = shift(partial, 0, -step)
        value = value + partial.astype(jnp.float32)
    hidden = jax.nn.silu(tie(value, rows_before, facts_before)).astype(jnp.bfloat16)
    edges = [SIDE * SIDE * sum(CUTS[:c]) for c in range(len(CUTS) + 1)]
    hiddens = [hidden[edges[c] : edges[c + 1]] for c in cuts]

    slot = facts_before[0].astype(jnp.int32)
    table = (slot[:, None] == lanes[None, :]).astype(jnp.bfloat16)
    gathered = []
    for c in cuts:
        sent = tie(hiddens[c], *gathered[0][1:]) if c else hiddens[c]
        gathered.append([shift(turn(sent, step, CUTS[c]), 0, step) if step else sent for step in range(SIDE)])

    combined = [0.0] * SIDE
    landed = []
    for c in cuts:
        out = 0.0
        for step in range(SIDE):
            out = out + jnp.dot(gathered[c][step], of(downs, -step), preferred_element_type=jnp.float32)
        out = out.astype(jnp.bfloat16).reshape(SIDE, SIDE, CUTS[c], PART)
        if c:
            returns = jnp.stack([
                lax.dynamic_index_in_dim(out, (y - target) % SIDE, 0, keepdims=False) for target in range(SIDE)
            ])
            back = tie(exchange(returns, along_y=True), ours, theirs).astype(jnp.float32)
            pairs = [back[0] + back[1], back[2] + back[3]]
            ours = jnp.where(own == 0, pairs[0], pairs[1]).astype(jnp.bfloat16)
            theirs = jnp.where(own == 0, pairs[1], pairs[0]).astype(jnp.bfloat16)
        else:
            back = [(shift(out[step], -step, 0) if step else out[0]).astype(jnp.float32) for step in range(SIDE)]
            ours = (back[0] + jnp.where(even, back[1], back[3])).astype(jnp.bfloat16)
            theirs = (back[2] + jnp.where(even, back[3], back[1])).astype(jnp.bfloat16)
        messages = [jnp.concatenate([ours[step], theirs[step]]) for step in range(SIDE)]
        if c:
            messages = [tie(message, *landed) for message in messages]
        landed = [shift_on(message, -step) for step, message in enumerate(messages)]
        chosen = table[:, starts[c] : starts[c] + EXPERTS * CUTS[c]]
        for step in range(SIDE):
            combined[step] = combined[step] + jnp.dot(chosen, landed[step], preferred_element_type=jnp.float32)

    result = jnp.zeros((count, D), jnp.bfloat16)
    for step in range(SIDE):
        part = lax.dynamic_slice(rows_before, (0, quarter(step)), (count, PART))
        updated = part.astype(jnp.float32) + facts_before[1][:, None] * combined[step]
        result = lax.dynamic_update_slice(result, updated.astype(jnp.bfloat16), (0, quarter(step)))
    return result.reshape(tokens.shape)


def solution(mesh):
    in_specs = (
        P("pipe", "expert", None),
        P("pipe", None, "expert"),
        P("pipe", "expert", None),
        P(None, "pipe", "expert", None),
        P(None, "pipe", "expert"),
    )
    out_specs = P("pipe", "expert", None)
    return jax.shard_map(
        per_device, mesh=mesh, in_specs=in_specs, out_specs=out_specs, check_vma=False
    )
```

```python
import jax
import jax.numpy as jnp
from jax import lax
from jax.sharding import PartitionSpec as P

D = 7168
EXPERTS = 2
CAP = 18
SIDE = 4
PART = D // SIDE
CUTS = (40, 32)

epsilon = 1e-06


def shift(block, dy, dx):
    pairs = []
    for y in range(SIDE):
        for x in range(SIDE):
            pairs.append((y * SIDE + x, (y + dy) % SIDE * SIDE + (x + dx) % SIDE))
    return lax.ppermute(block, "expert", pairs)


def shift_on(block, dx):
    count = lax.axis_size("pipe")
    pairs = []
    for p in range(count):
        for y in range(SIDE):
            for x in range(SIDE):
                source = p * SIDE * SIDE + y * SIDE + x
                target = (p + 1) % count * SIDE * SIDE + y * SIDE + (x + dx) % SIDE
                pairs.append((source, target))
    return lax.ppermute(block, ("pipe", "expert"), pairs)


def normalize(tok_rows):
    widened = tok_rows.astype(jnp.float32)
    inverse_rms = lax.rsqrt(jnp.mean(widened * widened, axis=-1, keepdims=True) + epsilon)
    return (widened * inverse_rms).astype(jnp.bfloat16)


def slots_of(ids, own):
    rel = (ids != own).astype(jnp.int32)
    count = ids.shape[0]
    member = (rel[:, None] == jnp.arange(EXPERTS, dtype=jnp.int32)[None, :]).astype(jnp.bfloat16)
    earlier = jnp.arange(count)[:, None] > jnp.arange(count)[None, :]
    before = jnp.dot(earlier.astype(jnp.bfloat16), member, preferred_element_type=jnp.float32)
    rank = jnp.sum(before * member.astype(jnp.float32), axis=1).astype(jnp.int32)
    slot, first = 0 * rank, 0
    for size in CUTS:
        inside = (rank >= first) & (rank < first + size)
        slot = jnp.where(inside, EXPERTS * first + rel * size + rank - first, slot)
        first += size
    return slot


def turn(block, step, slots):
    split = block.reshape(SIDE, SIDE, slots, -1)
    return jnp.roll(split, step, axis=1).reshape(block.shape)


def tie(value, *done):
    return lax.optimization_barrier((value, *done))[0]


def exchange(pieces, along_y=False):
    groups = [[y * SIDE + x for x in range(SIDE)] for y in range(SIDE)]
    if along_y:
        groups = [list(group) for group in zip(*groups)]
    return lax.all_to_all(pieces, "expert", 0, 0, axis_index_groups=groups, tiled=True)


def per_device(tokens, up_weight, down_weight, route, gates):
    ticks, _, block, _ = route.shape
    count = ticks * block
    assert sum(CUTS) == ticks * CAP
    place = lax.axis_index("expert")
    y, x = place // SIDE, place % SIDE
    even = y % 2 == 0
    own = y // 2
    up_local, down_local = up_weight[0], down_weight[0]
    depth = up_local.shape[1]
    rows = tokens.reshape(count, D)
    starts = [EXPERTS * sum(CUTS[:c]) for c in range(len(CUTS))]
    cuts = range(len(CUTS))

    def quarter(step):
        return (x + step) % SIDE * PART

    def of(pieces, step):
        return lax.dynamic_index_in_dim(pieces, (x + step) % SIDE, 0, keepdims=False)

    ups = exchange(up_local.reshape(SIDE, PART, depth))
    downs = exchange(jnp.transpose(down_local.reshape(depth, SIDE, PART), (1, 0, 2)))

    slot = slots_of(route.reshape(count), own)
    lanes = jnp.arange(EXPERTS * ticks * CAP, dtype=jnp.int32)
    table = (lanes[:, None] == slot[None, :]).astype(jnp.bfloat16)
    normed = normalize(rows)

    from_x = []
    for step in range(SIDE):
        part = lax.dynamic_slice(normed, (0, quarter(step)), (count, PART))
        message = jnp.dot(table, part, preferred_element_type=jnp.float32).astype(jnp.bfloat16)
        from_x.append(shift(message, 0, step) if step else message)

    received = []
    for c in cuts:
        ours = jnp.stack([r[starts[c] : starts[c] + CUTS[c]] for r in from_x])
        theirs = jnp.stack([r[starts[c] + CUTS[c] : starts[c] + EXPERTS * CUTS[c]] for r in from_x])
        if c:
            ours = tie(ours, ups)
            theirs = tie(theirs, ups)
        sent = [ours, jnp.where(even, ours, theirs), theirs, jnp.where(even, theirs, ours)]
        from_y = [shift(m, step, 0) if step else m for step, m in enumerate(sent)]
        received.append(jnp.stack(from_y).reshape(-1, PART))

    facts = jnp.stack([slot.astype(jnp.float32), gates.reshape(count)])
    rows_before = shift_on(tie(rows, received[0]), 0)
    facts_before = shift_on(tie(facts, received[0]), 0)

    value = 0.0
    for step in range(SIDE):
        partial = []
        for c in cuts:
            product = jnp.dot(received[c], of(ups, -step), preferred_element_type=jnp.float32)
            partial.append(turn(product.astype(jnp.bfloat16), -step, CUTS[c]) if step else product)
        partial = jnp.concatenate(partial)
        if step:
            partial = shift(partial, 0, -step)
        value = value + partial.astype(jnp.float32)
    hidden = jax.nn.silu(tie(value, rows_before, facts_before)).astype(jnp.bfloat16)
    edges = [SIDE * SIDE * sum(CUTS[:c]) for c in range(len(CUTS) + 1)]
    hiddens = [hidden[edges[c] : edges[c + 1]] for c in cuts]

    slot = facts_before[0].astype(jnp.int32)
    table = (slot[:, None] == lanes[None, :]).astype(jnp.bfloat16)
    gathered = []
    for c in cuts:
        sent = tie(hiddens[c], gathered[0][2]) if c else hiddens[c]
        gathered.append([shift(turn(sent, step, CUTS[c]), 0, step) if step else sent for step in range(SIDE)])

    downs = tie(downs, hidden)
    down = jnp.concatenate([of(downs, -step) for step in range(SIDE)])

    combined = [0.0] * SIDE
    landed = []
    for c in cuts:
        out = jnp.dot(jnp.concatenate(gathered[c], axis=1), down, preferred_element_type=jnp.float32)
        out = out.astype(jnp.bfloat16).reshape(SIDE, SIDE, CUTS[c], PART)
        if c:
            returns = jnp.stack([
                lax.dynamic_index_in_dim(out, (y - target) % SIDE, 0, keepdims=False) for target in range(SIDE)
            ])
            back = tie(exchange(returns, along_y=True), ours, theirs).astype(jnp.float32)
            pairs = [back[0] + back[1], back[2] + back[3]]
            ours = jnp.where(own == 0, pairs[0], pairs[1]).astype(jnp.bfloat16)
            theirs = jnp.where(own == 0, pairs[1], pairs[0]).astype(jnp.bfloat16)
        else:
            back = [(shift(out[step], -step, 0) if step else out[0]).astype(jnp.float32) for step in range(SIDE)]
            ours = (back[0] + jnp.where(even, back[1], back[3])).astype(jnp.bfloat16)
            theirs = (back[2] + jnp.where(even, back[3], back[1])).astype(jnp.bfloat16)
        messages = [jnp.concatenate([ours[step], theirs[step]]) for step in range(SIDE)]
        if c:
            messages = [tie(message, *landed) for message in messages]
        landed = [shift_on(message, -step) for step, message in enumerate(messages)]
        chosen = table[:, starts[c] : starts[c] + EXPERTS * CUTS[c]]
        for step in range(SIDE):
            combined[step] = combined[step] + jnp.dot(chosen, landed[step], preferred_element_type=jnp.float32)

    result = jnp.zeros((count, D), jnp.bfloat16)
    for step in range(SIDE):
        part = lax.dynamic_slice(rows_before, (0, quarter(step)), (count, PART))
        updated = part.astype(jnp.float32) + facts_before[1][:, None] * combined[step]
        result = lax.dynamic_update_slice(result, updated.astype(jnp.bfloat16), (0, quarter(step)))
    return result.reshape(tokens.shape)


def solution(mesh):
    in_specs = (
        P("pipe", "expert", None),
        P("pipe", None, "expert"),
        P("pipe", "expert", None),
        P(None, "pipe", "expert", None),
        P(None, "pipe", "expert"),
    )
    out_specs = P("pipe", "expert", None)
    return jax.shard_map(
        per_device, mesh=mesh, in_specs=in_specs, out_specs=out_specs, check_vma=False
    )
```

```python
import jax
import jax.numpy as jnp
from jax import lax
from jax.sharding import PartitionSpec as P

D = 7168
EXPERTS = 2
CAP = 18
SIDE = 4
PART = D // SIDE
CUTS = (40, 32)

epsilon = 1e-06


def shift(block, dy, dx):
    pairs = []
    for y in range(SIDE):
        for x in range(SIDE):
            pairs.append((y * SIDE + x, (y + dy) % SIDE * SIDE + (x + dx) % SIDE))
    return lax.ppermute(block, "expert", pairs)


def shift_on(block, dx):
    count = lax.axis_size("pipe")
    pairs = []
    for p in range(count):
        for y in range(SIDE):
            for x in range(SIDE):
                source = p * SIDE * SIDE + y * SIDE + x
                target = (p + 1) % count * SIDE * SIDE + y * SIDE + (x + dx) % SIDE
                pairs.append((source, target))
    return lax.ppermute(block, ("pipe", "expert"), pairs)


def inverse_rms(tok_rows):
    widened = tok_rows.astype(jnp.float32)
    return lax.rsqrt(jnp.mean(widened * widened, axis=-1, keepdims=True) + epsilon)


def slots_of(ids, own):
    rel = (ids != own).astype(jnp.int32)
    count = ids.shape[0]
    member = (rel[:, None] == jnp.arange(EXPERTS, dtype=jnp.int32)[None, :]).astype(jnp.bfloat16)
    earlier = jnp.arange(count)[:, None] > jnp.arange(count)[None, :]
    before = jnp.dot(earlier.astype(jnp.bfloat16), member, preferred_element_type=jnp.float32)
    rank = jnp.sum(before * member.astype(jnp.float32), axis=1).astype(jnp.int32)
    slot, first = 0 * rank, 0
    for size in CUTS:
        inside = (rank >= first) & (rank < first + size)
        slot = jnp.where(inside, EXPERTS * first + rel * size + rank - first, slot)
        first += size
    return slot


def turn(block, step, slots):
    split = block.reshape(SIDE, SIDE, slots, -1)
    return jnp.roll(split, step, axis=1).reshape(block.shape)


def tie(value, *done):
    return lax.optimization_barrier((value, *done))[0]


def exchange(pieces, along_y=False):
    groups = [[y * SIDE + x for x in range(SIDE)] for y in range(SIDE)]
    if along_y:
        groups = [list(group) for group in zip(*groups)]
    return lax.all_to_all(pieces, "expert", 0, 0, axis_index_groups=groups, tiled=True)


def per_device(tokens, up_weight, down_weight, route, gates):
    ticks, _, block, _ = route.shape
    count = ticks * block
    assert sum(CUTS) == ticks * CAP
    place = lax.axis_index("expert")
    y, x = place // SIDE, place % SIDE
    even = y % 2 == 0
    own = y // 2
    up_local, down_local = up_weight[0], down_weight[0]
    depth = up_local.shape[1]
    rows = tokens.reshape(count, D)
    starts = [EXPERTS * sum(CUTS[:c]) for c in range(len(CUTS))]
    cuts = range(len(CUTS))

    def quarter(step):
        return (x + step) % SIDE * PART

    def of(pieces, step):
        return lax.dynamic_index_in_dim(pieces, (x + step) % SIDE, 0, keepdims=False)

    ups = exchange(up_local.reshape(SIDE, PART, depth))
    downs = exchange(jnp.transpose(down_local.reshape(depth, SIDE, PART), (1, 0, 2)))

    slot = slots_of(route.reshape(count), own)
    lanes = jnp.arange(EXPERTS * ticks * CAP, dtype=jnp.int32)
    table = (lanes[:, None] == slot[None, :]).astype(jnp.bfloat16)
    scale = inverse_rms(rows)

    from_x = []
    for step in range(SIDE):
        part = lax.dynamic_slice(rows, (0, quarter(step)), (count, PART))
        part = (part.astype(jnp.float32) * scale).astype(jnp.bfloat16)
        message = jnp.dot(table, part, preferred_element_type=jnp.float32).astype(jnp.bfloat16)
        from_x.append(shift(message, 0, step) if step else message)

    received = []
    for c in cuts:
        ours = jnp.stack([r[starts[c] : starts[c] + CUTS[c]] for r in from_x])
        theirs = jnp.stack([r[starts[c] + CUTS[c] : starts[c] + EXPERTS * CUTS[c]] for r in from_x])
        if c:
            ours = tie(ours, ups)
            theirs = tie(theirs, ups)
        sent = [ours, jnp.where(even, ours, theirs), theirs, jnp.where(even, theirs, ours)]
        from_y = [shift(m, step, 0) if step else m for step, m in enumerate(sent)]
        received.append(jnp.stack(from_y).reshape(-1, PART))

    facts = jnp.stack([slot.astype(jnp.float32), gates.reshape(count)])
    rows_before = shift_on(tie(rows, received[0]), 0)
    facts_before = shift_on(tie(facts, received[0]), 0)

    value = 0.0
    for step in range(SIDE):
        partial = []
        for c in cuts:
            product = jnp.dot(received[c], of(ups, -step), preferred_element_type=jnp.float32)
            partial.append(turn(product.astype(jnp.bfloat16), -step, CUTS[c]) if step else product)
        partial = jnp.concatenate(partial)
        if step:
            partial = shift(partial, 0, -step)
        value = value + partial.astype(jnp.float32)
    hidden = jax.nn.silu(tie(value, rows_before, facts_before)).astype(jnp.bfloat16)
    edges = [SIDE * SIDE * sum(CUTS[:c]) for c in range(len(CUTS) + 1)]
    hiddens = [hidden[edges[c] : edges[c + 1]] for c in cuts]

    slot = facts_before[0].astype(jnp.int32)
    table = (slot[:, None] == lanes[None, :]).astype(jnp.bfloat16)
    gathered = []
    for c in cuts:
        sent = tie(hiddens[c], *gathered[0][1:]) if c else hiddens[c]
        gathered.append([shift(turn(sent, step, CUTS[c]), 0, step) if step else sent for step in range(SIDE)])

    result = rows_before
    landed = []
    for c in cuts:
        out = 0.0
        for step in range(SIDE):
            out = out + jnp.dot(gathered[c][step], of(downs, -step), preferred_element_type=jnp.float32)
        out = out.astype(jnp.bfloat16).reshape(SIDE, SIDE, CUTS[c], PART)
        if c:
            returns = jnp.stack([
                lax.dynamic_index_in_dim(out, (y - target) % SIDE, 0, keepdims=False) for target in range(SIDE)
            ])
            back = tie(exchange(returns, along_y=True), ours, theirs).astype(jnp.float32)
            pairs = [back[0] + back[1], back[2] + back[3]]
            ours = jnp.where(own == 0, pairs[0], pairs[1]).astype(jnp.bfloat16)
            theirs = jnp.where(own == 0, pairs[1], pairs[0]).astype(jnp.bfloat16)
        else:
            back = [(shift(out[step], -step, 0) if step else out[0]).astype(jnp.float32) for step in range(SIDE)]
            ours = (back[0] + jnp.where(even, back[1], back[3])).astype(jnp.bfloat16)
            theirs = (back[2] + jnp.where(even, back[3], back[1])).astype(jnp.bfloat16)
        messages = [jnp.concatenate([ours[step], theirs[step]]) for step in range(SIDE)]
        if c:
            messages = [tie(message, *landed) for message in messages]
        landed = [shift_on(message, -step) for step, message in enumerate(messages)]
        chosen = table[:, starts[c] : starts[c] + EXPERTS * CUTS[c]]
        for step in range(SIDE):
            combined = jnp.dot(chosen, landed[step], preferred_element_type=jnp.float32)
            part = lax.dynamic_slice(result, (0, quarter(step)), (count, PART))
            updated = part.astype(jnp.float32) + facts_before[1][:, None] * combined
            result = lax.dynamic_update_slice(result, updated.astype(jnp.bfloat16), (0, quarter(step)))

    return result.reshape(tokens.shape)


def solution(mesh):
    in_specs = (
        P("pipe", "expert", None),
        P("pipe", None, "expert"),
        P("pipe", "expert", None),
        P(None, "pipe", "expert", None),
        P(None, "pipe", "expert"),
    )
    out_specs = P("pipe", "expert", None)
    return jax.shard_map(
        per_device, mesh=mesh, in_specs=in_specs, out_specs=out_specs, check_vma=False
    )
```

```python
import jax
import jax.numpy as jnp
from jax import lax
from jax.sharding import PartitionSpec as P

D = 7168
EXPERTS = 2
CAP = 18
SIDE = 4
PART = D // SIDE
CUTS = (40, 32)

epsilon = 1e-06


def shift(block, dy, dx):
    pairs = []
    for y in range(SIDE):
        for x in range(SIDE):
            pairs.append((y * SIDE + x, (y + dy) % SIDE * SIDE + (x + dx) % SIDE))
    return lax.ppermute(block, "expert", pairs)


def shift_on(block, dx):
    count = lax.axis_size("pipe")
    pairs = []
    for p in range(count):
        for y in range(SIDE):
            for x in range(SIDE):
                source = p * SIDE * SIDE + y * SIDE + x
                target = (p + 1) % count * SIDE * SIDE + y * SIDE + (x + dx) % SIDE
                pairs.append((source, target))
    return lax.ppermute(block, ("pipe", "expert"), pairs)


def inverse_rms(tok_rows):
    widened = tok_rows.astype(jnp.float32)
    return lax.rsqrt(jnp.mean(widened * widened, axis=-1, keepdims=True) + epsilon)


def slots_of(ids, own):
    rel = (ids != own).astype(jnp.int32)
    count = ids.shape[0]
    member = (rel[:, None] == jnp.arange(EXPERTS, dtype=jnp.int32)[None, :]).astype(jnp.bfloat16)
    earlier = jnp.arange(count)[:, None] > jnp.arange(count)[None, :]
    before = jnp.dot(earlier.astype(jnp.bfloat16), member, preferred_element_type=jnp.float32)
    rank = jnp.sum(before * member.astype(jnp.float32), axis=1).astype(jnp.int32)
    slot, first = 0 * rank, 0
    for size in CUTS:
        inside = (rank >= first) & (rank < first + size)
        slot = jnp.where(inside, EXPERTS * first + rel * size + rank - first, slot)
        first += size
    return slot


def turn(block, step, slots):
    split = block.reshape(SIDE, SIDE, slots, -1)
    return jnp.roll(split, step, axis=1).reshape(block.shape)


def tie(value, *done):
    return lax.optimization_barrier((value, *done))[0]


def exchange(pieces, along_y=False):
    groups = [[y * SIDE + x for x in range(SIDE)] for y in range(SIDE)]
    if along_y:
        groups = [list(group) for group in zip(*groups)]
    return lax.all_to_all(pieces, "expert", 0, 0, axis_index_groups=groups, tiled=True)


def per_device(tokens, up_weight, down_weight, route, gates):
    ticks, _, block, _ = route.shape
    count = ticks * block
    assert sum(CUTS) == ticks * CAP
    place = lax.axis_index("expert")
    y, x = place // SIDE, place % SIDE
    even = y % 2 == 0
    own = y // 2
    up_local, down_local = up_weight[0], down_weight[0]
    depth = up_local.shape[1]
    rows = tokens.reshape(count, D)
    starts = [EXPERTS * sum(CUTS[:c]) for c in range(len(CUTS))]
    cuts = range(len(CUTS))

    def quarter(step):
        return (x + step) % SIDE * PART

    def of(pieces, step):
        return lax.dynamic_index_in_dim(pieces, (x + step) % SIDE, 0, keepdims=False)

    ups = exchange(up_local.reshape(SIDE, PART, depth))
    downs = exchange(jnp.transpose(down_local.reshape(depth, SIDE, PART), (1, 0, 2)))

    slot = slots_of(route.reshape(count), own)
    lanes = jnp.arange(EXPERTS * ticks * CAP, dtype=jnp.int32)
    table = (lanes[:, None] == slot[None, :]).astype(jnp.bfloat16)
    scale = inverse_rms(rows)

    from_x = []
    for step in range(SIDE):
        part = lax.dynamic_slice(rows, (0, quarter(step)), (count, PART))
        part = (part.astype(jnp.float32) * scale).astype(jnp.bfloat16)
        message = jnp.dot(table, part, preferred_element_type=jnp.float32).astype(jnp.bfloat16)
        from_x.append(shift(message, 0, step) if step else message)

    received = []
    for c in cuts:
        ours = jnp.stack([r[starts[c] : starts[c] + CUTS[c]] for r in from_x])
        theirs = jnp.stack([r[starts[c] + CUTS[c] : starts[c] + EXPERTS * CUTS[c]] for r in from_x])
        if c:
            ours = tie(ours, ups)
            theirs = tie(theirs, ups)
        sent = [ours, jnp.where(even, ours, theirs), theirs, jnp.where(even, theirs, ours)]
        from_y = [shift(m, step, 0) if step else m for step, m in enumerate(sent)]
        received.append(jnp.stack(from_y).reshape(-1, PART))

    facts = jnp.stack([slot.astype(jnp.float32), gates.reshape(count)])
    rows_before = shift_on(tie(rows, received[0]), 0)
    facts_before = shift_on(tie(facts, received[0]), 0)

    value = 0.0
    for step in range(SIDE):
        partial = []
        for c in cuts:
            product = jnp.dot(received[c], of(ups, -step), preferred_element_type=jnp.float32)
            partial.append(turn(product.astype(jnp.bfloat16), -step, CUTS[c]) if step else product)
        partial = jnp.concatenate(partial)
        if step:
            partial = shift(partial, 0, -step)
        value = value + partial.astype(jnp.float32)
    hidden = jax.nn.silu(tie(value, rows_before, facts_before)).astype(jnp.bfloat16)
    edges = [SIDE * SIDE * sum(CUTS[:c]) for c in range(len(CUTS) + 1)]
    hiddens = [hidden[edges[c] : edges[c + 1]] for c in cuts]

    slot = facts_before[0].astype(jnp.int32)
    table = (slot[:, None] == lanes[None, :]).astype(jnp.bfloat16)
    gathered = []
    for c in cuts:
        sent = tie(hiddens[c], *gathered[0][1:]) if c else hiddens[c]
        gathered.append([shift(turn(sent, step, CUTS[c]), 0, step) if step else sent for step in range(SIDE)])

    result = rows_before
    landed = []
    for c in cuts:
        out = 0.0
        for step in range(SIDE):
            out = out + jnp.dot(gathered[c][step], of(downs, -step), preferred_element_type=jnp.float32)
        out = out.astype(jnp.bfloat16).reshape(SIDE, SIDE, CUTS[c], PART)
        if c:
            returns = jnp.stack([
                lax.dynamic_index_in_dim(out, (y - target) % SIDE, 0, keepdims=False) for target in range(SIDE)
            ])
            back = tie(exchange(returns, along_y=True), ours, theirs).astype(jnp.float32)
            pairs = [back[0] + back[1], back[2] + back[3]]
            ours = jnp.where(own == 0, pairs[0], pairs[1]).astype(jnp.bfloat16)
            theirs = jnp.where(own == 0, pairs[1], pairs[0]).astype(jnp.bfloat16)
        else:
            back = [(shift(out[step], -step, 0) if step else out[0]).astype(jnp.float32) for step in range(SIDE)]
            ours = (back[0] + jnp.where(even, back[1], back[3])).astype(jnp.bfloat16)
            theirs = (back[2] + jnp.where(even, back[3], back[1])).astype(jnp.bfloat16)
        messages = [jnp.concatenate([ours[step], theirs[step]]) for step in range(SIDE)]
        landed.append([shift_on(message, -step) for step, message in enumerate(messages)])
    for c in cuts:
        chosen = table[:, starts[c] : starts[c] + EXPERTS * CUTS[c]]
        for step in range(SIDE):
            arrived = landed[c][step] if c else tie(landed[c][step], *messages)
            combined = jnp.dot(chosen, arrived, preferred_element_type=jnp.float32)
            part = lax.dynamic_slice(result, (0, quarter(step)), (count, PART))
            updated = part.astype(jnp.float32) + facts_before[1][:, None] * combined
            result = lax.dynamic_update_slice(result, updated.astype(jnp.bfloat16), (0, quarter(step)))

    return result.reshape(tokens.shape)


def solution(mesh):
    in_specs = (
        P("pipe", "expert", None),
        P("pipe", None, "expert"),
        P("pipe", "expert", None),
        P(None, "pipe", "expert", None),
        P(None, "pipe", "expert"),
    )
    out_specs = P("pipe", "expert", None)
    return jax.shard_map(
        per_device, mesh=mesh, in_specs=in_specs, out_specs=out_specs, check_vma=False
    )
```
